32 devices in a mesh: row: 8 (over y, x, core), col: 4 (over z).
Axes of the slice: x: 2, y: 2, z: 4, core: 2. Of those that a mesh axis runs over, the one named last changes fastest.
Arguments:
- precision: float32 [16384, 16384], P('row', 'col'), may hold values from -0.3 to 4, as said below
- samples: bfloat16 [1024, 16384], P(None, 'col'), may hold values from -6 to 6
- step_size: float32 [1], replicated, may hold values from 0.5 to 1
- threshold: float32 [1], replicated, may hold values from 0.1 to 0.3
Outputs:
- updated: float32 [16384, 16384], P('row', 'col')
The draws below stay inside these ranges and needn't reach their ends.
Inputs may be any that keep to these rules, and one draw needn't show every extreme that they name: precision is symmetric; its diagonal entries lie between 1 and 4.
All inputs are finite; a program needn't handle non-finite values.
Results may differ from the reference program's by a relative error of at most 0.0056.
Values may be sent and summed in bfloat16 or wider, within the bound.
A program may use at most 192 MiB of HBM per device.

```python
import math
import jax
import jax.numpy as jnp
from jax import lax

P_SIZE = 16384
NSAMP = 1024
N_ROW = 8


def draw_precision(key, part):
    first_key = jax.random.fold_in(key, 11)
    second_key = jax.random.fold_in(key, 12)
    spread = jnp.clip(0.05 * jax.random.normal(first_key, (P_SIZE, P_SIZE), jnp.float32), -0.3, 0.3)
    spread = 0.5 * (spread + spread.T)
    diag_values = jnp.exp(jax.random.uniform(second_key, (P_SIZE,), jnp.float32, 0.0, math.log(4.0)))
    indices = jnp.arange(P_SIZE, dtype=jnp.int32)
    on_diagonal = indices[:, None] == indices[None, :]
    return jnp.where(on_diagonal, diag_values[:, None], spread)


def block_levels(key, extent, pieces, smallest, high):
    loudness, own = 1.0, jax.random.fold_in(key, 6)
    for dim, parts in pieces:
        heights = jnp.exp(jax.random.uniform(jax.random.fold_in(own, dim), (parts,), jnp.float32, smallest / len(pieces), high / len(pieces)))
        loudness = loudness * jnp.repeat(heights, extent[dim] // parts).reshape([-1 if axis == dim else 1 for axis in range(len(extent))])
    return loudness


def scatter_about(own_key, shape, width, most, pieces=(), held_as=jnp.bfloat16):
    entries = width * jax.random.normal(own_key, shape, jnp.float32)
    if pieces:
        entries = entries * block_levels(own_key, shape, pieces, -0.22, 0.18)
    return jnp.clip(entries, -most, most).astype(held_as)


def setup_inputs(seed: int = 0) -> dict:
    arg_keys = jax.random.split(jax.random.key(seed), 5)
    return {
        "precision": draw_precision(jax.random.fold_in(arg_keys[4], 71), 0),
        "samples": scatter_about(arg_keys[1], (NSAMP, P_SIZE), 1.0, 6.0, ((1, 4),)),
        "step_size": jnp.clip(jax.random.uniform(arg_keys[2], (1,), jnp.float32, 0.5, 1.0), 0.5, 1.0),
        "threshold": jnp.clip(jax.random.uniform(arg_keys[3], (1,), jnp.float32, 0.1, 0.3), 0.1, 0.3),
    }


def reference(precision, samples, step_size, threshold):
    sample_count = samples.shape[0]
    rounded = precision.astype(jnp.bfloat16)
    projected = lax.dot_general(samples, rounded, (((1,), (1,)), ((), ())), preferred_element_type=jnp.float32).astype(jnp.bfloat16)
    band_rows = P_SIZE // N_ROW
    all_cols = jnp.arange(P_SIZE, dtype=jnp.int32)

    def one_band(index):
        offset_row = (index * band_rows).astype(jnp.int32)
        proj_band = lax.dynamic_slice_in_dim(projected, offset_row, band_rows, 1)
        data_band = lax.dynamic_slice_in_dim(samples, offset_row, band_rows, 1)
        cross_rows = lax.dot_general(proj_band, samples, (((0,), (0,)), ((), ())), preferred_element_type=jnp.float32) / sample_count
        cross_cols = lax.dot_general(data_band, projected, (((0,), (0,)), ((), ())), preferred_element_type=jnp.float32) / sample_count
        symmetric = 0.5 * (cross_rows + cross_cols)
        current = lax.dynamic_slice_in_dim(precision, offset_row, band_rows, 0)
        global_row = offset_row + jnp.arange(band_rows, dtype=jnp.int32)
        on_diagonal = global_row[:, None] == all_cols[None, :]
        gradient = symmetric - jnp.where(on_diagonal, 1.0 / jnp.where(on_diagonal, current, 1.0), 0.0)
        stepped = current - step_size[0] * gradient
        shrunk = jnp.sign(stepped) * jnp.maximum(jnp.abs(stepped) - step_size[0] * threshold[0], 0.0)
        return jnp.where(on_diagonal, stepped, shrunk)

    bands = lax.map(one_band, jnp.arange(N_ROW, dtype=jnp.int32))
    return bands.reshape(P_SIZE, P_SIZE)
```

```python
import functools

import jax
import jax.numpy as jnp
from jax import lax
from jax.experimental import pallas as pl
from jax.experimental.pallas import tpu as pltpu
from jax.sharding import PartitionSpec as P

MESH = pl.DeviceIdType.MESH
PARTS = 2


def ring_place(group, groups):
    place = jnp.int32(0)
    for spot in range(groups):
        place = jnp.where(group == (spot ^ (spot >> 1)), spot, place)
    return place


def ring_group(place, groups):
    group = jnp.int32(0)
    for spot in range(groups):
        group = jnp.where(place == spot, spot ^ (spot >> 1), group)
    return group


def spread_kernel(
    row_count,
    col_count,
    block_ref,
    own_ref,
    samples_ref,
    left_ref,
    right_ref,
    gather_send,
    gather_recv,
    ring_send,
    ring_recv,
    core_send,
    core_recv,
    local_sem,
    step_sem,
):
    row, col = lax.axis_index("row"), lax.axis_index("col")
    ratio = row_count // col_count
    groups = col_count
    group, core = row // ratio, row % ratio
    depth, rows_tile = block_ref.shape
    total = samples_ref.shape[0]
    place = ring_place(group, groups)
    behind = lax.rem(place - ring_place(col, groups) + groups, groups)
    ahead = lax.rem(groups - behind, groups)
    next_row = ring_group(lax.rem(place + 1, groups), groups) * ratio + core
    last_row = ring_group(lax.rem(place + groups - 1, groups), groups) * ratio + core
    is_root = behind == 0

    peers = [(row, lax.rem(col + step, col_count)) for step in range(1, col_count)]
    peers += [(next_row, col), (last_row, col)]
    peers += [(group * ratio + lax.rem(core + step, ratio), col) for step in range(1, ratio)]
    barrier = pltpu.get_barrier_semaphore()
    for peer in peers:
        pl.semaphore_signal(barrier, inc=1, device_id=peer, device_id_type=MESH)
    pl.semaphore_wait(barrier, len(peers))

    part = depth // PARTS
    columns = pl.ds(pl.multiple_of(core * rows_tile, 128), rows_tile)

    def rows_of(step, piece, start):
        holder = lax.rem(col + step, col_count)
        return pl.ds(pl.multiple_of(start + holder * depth + piece * part, 16), part)

    def gather(step, piece):
        mine = rows_of(0, piece, 0)
        return pltpu.make_async_remote_copy(
            src_ref=block_ref.at[pl.ds(piece * part, part), :],
            dst_ref=left_ref.at[mine, :],
            send_sem=gather_send.at[step, piece],
            recv_sem=gather_recv.at[step, piece],
            device_id=(row, lax.rem(col - step + col_count, col_count)),
            device_id_type=MESH,
        )

    def arrival(step, piece):
        theirs = left_ref.at[rows_of(step, piece, 0), :]
        return pltpu.make_async_remote_copy(
            src_ref=theirs,
            dst_ref=theirs,
            send_sem=gather_send.at[step, piece],
            recv_sem=gather_recv.at[step, piece],
            device_id=(row, lax.rem(col - step + col_count, col_count)),
            device_id_type=MESH,
        )

    def ring(step, piece):
        held = right_ref.at[rows_of(step, piece, total), columns]
        return pltpu.make_async_remote_copy(
            src_ref=held,
            dst_ref=held,
            send_sem=ring_send.at[step, piece],
            recv_sem=ring_recv.at[step, piece],
            device_id=(next_row if (step + piece) % 2 == 0 else last_row, col),
            device_id_type=MESH,
        )

    def across(step, piece, hop, incoming):
        from_core = lax.rem(core + ratio - hop, ratio) if incoming else core
        there = pl.ds(pl.multiple_of(from_core * rows_tile, 128), rows_tile)
        held = right_ref.at[rows_of(step, piece, total), there]
        return pltpu.make_async_remote_copy(
            src_ref=held,
            dst_ref=held,
            send_sem=core_send.at[hop, step, piece],
            recv_sem=core_recv.at[hop, step, piece],
            device_id=(group * ratio + lax.rem(core + hop, ratio), col),
            device_id_type=MESH,
        )

    for piece in range(PARTS):
        for step in range(1, col_count):
            gather(step, piece).start()
    own_rows = pl.ds(pl.multiple_of(col * depth, 16), depth)
    local = [
        pltpu.make_async_copy(block_ref, left_ref.at[own_rows, :], local_sem.at[0]),
        pltpu.make_async_copy(own_ref, left_ref.at[pl.ds(total, total), :], local_sem.at[1]),
        pltpu.make_async_copy(samples_ref, right_ref.at[pl.ds(0, total), :], local_sem.at[2]),
    ]
    for copy in local:
        copy.start()

    for step in range(col_count):
        for piece in range(PARTS):
            travelled = behind if (step + piece) % 2 == 0 else ahead

            @pl.when(is_root)
            def _():
                if step == 0:
                    source = block_ref.at[pl.ds(piece * part, part), :]
                else:
                    arrival(step, piece).wait_recv()
                    source = left_ref.at[rows_of(step, piece, 0), :]
                copy = pltpu.make_async_copy(
                    source, right_ref.at[rows_of(step, piece, total), columns], step_sem.at[0]
                )
                copy.start()
                copy.wait()

            @pl.when(jnp.logical_not(is_root))
            def _():
                ring(step, piece).wait_recv()

            @pl.when(travelled < groups - 1)
            def _():
                ring(step, piece).start()

            for hop in range(1, ratio):
                across(step, piece, hop, False).start()

    for step in range(col_count):
        for piece in range(PARTS):
            travelled = behind if (step + piece) % 2 == 0 else ahead

            @pl.when(travelled < groups - 1)
            def _():
                ring(step, piece).wait_send()

            if step:
                @pl.when(jnp.logical_not(is_root))
                def _():
                    arrival(step, piece).wait_recv()

                gather(step, piece).wait_send()
            for hop in range(1, ratio):
                across(step, piece, hop, False).wait_send()
                across(step, piece, hop, True).wait_recv()
    for copy in local:
        copy.wait()


def spread(block, own, samples, row_count, col_count):
    total, cols_tile = samples.shape
    rows_tile = own.shape[1]
    ratio = row_count // col_count
    anywhere = pl.BlockSpec(memory_space=pl.ANY)
    pair = pltpu.SemaphoreType.DMA((col_count, PARTS))
    triple = pltpu.SemaphoreType.DMA((ratio, col_count, PARTS))
    return pl.pallas_call(
        functools.partial(spread_kernel, row_count, col_count),
        out_shape=(
            jax.ShapeDtypeStruct((2 * total, rows_tile), jnp.bfloat16),
            jax.ShapeDtypeStruct((2 * total, cols_tile), jnp.bfloat16),
        ),
        in_specs=[anywhere] * 3,
        out_specs=(anywhere, anywhere),
        scratch_shapes=[
            pair,
            pair,
            pair,
            pair,
            triple,
            triple,
            pltpu.SemaphoreType.DMA((3,)),
            pltpu.SemaphoreType.DMA((1,)),
        ],
        compiler_params=pltpu.CompilerParams(collective_id=0, has_side_effects=True),
    )(block, own, samples)


def per_device(precision, samples, step_size, threshold):
    rows_tile, cols_tile = precision.shape
    sample_count = samples.shape[0]
    row_count, col_count = lax.axis_size("row"), lax.axis_size("col")
    row_index, col_index = lax.axis_index("row"), lax.axis_index("col")
    share = sample_count // row_count
    piece = lax.dynamic_slice_in_dim(samples, row_index * share, share, 0)
    panel = lax.all_gather(piece, "col", axis=1, tiled=True)
    own_samples = lax.all_to_all(panel, "row", split_axis=1, concat_axis=0, tiled=True)

    depth = sample_count // col_count
    rounded = precision.astype(jnp.bfloat16)
    partial = lax.dot_general(
        samples, rounded, (((1,), (1,)), ((), ())), preferred_element_type=jnp.float32
    ).astype(jnp.bfloat16)
    terms = lax.all_to_all(
        partial.reshape(col_count, depth, rows_tile), "col", split_axis=0, concat_axis=0
    )
    block = jnp.sum(terms.astype(jnp.float32), axis=0).astype(jnp.bfloat16)

    left, right = spread(block, own_samples, samples, row_count, col_count)
    symmetric = lax.dot_general(
        left, right, (((0,), (0,)), ((), ())), preferred_element_type=jnp.float32
    ) * (0.5 / sample_count)
    global_row = row_index * rows_tile + jnp.arange(rows_tile, dtype=jnp.int32)
    global_col = col_index * cols_tile + jnp.arange(cols_tile, dtype=jnp.int32)
    on_diagonal = global_row[:, None] == global_col[None, :]
    gradient = symmetric - jnp.where(on_diagonal, 1.0 / jnp.where(on_diagonal, precision, 1.0), 0.0)
    stepped = precision - step_size[0] * gradient
    shrunk = jnp.sign(stepped) * jnp.maximum(jnp.abs(stepped) - step_size[0] * threshold[0], 0.0)
    return jnp.where(on_diagonal, stepped, shrunk)


def solution(mesh):
    in_specs = (P("row", "col"), P(None, "col"), P(), P())
    out_specs = P("row", "col")
    return jax.shard_map(
        per_device, mesh=mesh, in_specs=in_specs, out_specs=out_specs, check_vma=False
    )
```

```python
import functools

import jax
import jax.numpy as jnp
from jax import lax
from jax.experimental import pallas as pl
from jax.experimental.pallas import tpu as pltpu
from jax.sharding import PartitionSpec as P

MESH = pl.DeviceIdType.MESH
PARTS = 2


def ring_place(group, groups):
    place = jnp.int32(0)
    for spot in range(groups):
        place = jnp.where(group == (spot ^ (spot >> 1)), spot, place)
    return place


def ring_group(place, groups):
    group = jnp.int32(0)
    for spot in range(groups):
        group = jnp.where(place == spot, spot ^ (spot >> 1), group)
    return group


def spread_kernel(
    row_count,
    col_count,
    block_ref,
    panel_ref,
    samples_ref,
    left_ref,
    right_ref,
    gather_send,
    gather_recv,
    ring_send,
    ring_recv,
    core_send,
    core_recv,
    deal_send,
    deal_recv,
    load_sem,
    store_sem,
    step_sem,
    block_held,
    own_held,
    samples_held,
    part_held,
):
    row, col = lax.axis_index("row"), lax.axis_index("col")
    ratio = row_count // col_count
    groups = col_count
    group, core = row // ratio, row % ratio
    depth, rows_tile = block_ref.shape
    total = samples_ref.shape[0]
    place = ring_place(group, groups)
    behind = lax.rem(place - ring_place(col, groups) + groups, groups)
    ahead = lax.rem(groups - behind, groups)
    next_row = ring_group(lax.rem(place + 1, groups), groups) * ratio + core
    last_row = ring_group(lax.rem(place + groups - 1, groups), groups) * ratio + core
    is_root = behind == 0

    peers = [(row, lax.rem(col + step, col_count)) for step in range(1, col_count)]
    peers += [(lax.rem(row + step, row_count), col) for step in range(1, row_count)]
    barrier = pltpu.get_barrier_semaphore()
    for peer in peers:
        pl.semaphore_signal(barrier, inc=1, device_id=peer, device_id_type=MESH)
    pl.semaphore_wait(barrier, len(peers))

    part = depth // PARTS
    columns = pl.ds(pl.multiple_of(core * rows_tile, 128), rows_tile)

    def rows_of(step, piece, start):
        holder = lax.rem(col + step, col_count)
        return pl.ds(pl.multiple_of(start + holder * depth + piece * part, 16), part)

    def gather(step, piece):
        mine = rows_of(0, piece, 0)
        return pltpu.make_async_remote_copy(
            src_ref=block_ref.at[pl.ds(piece * part, part), :],
            dst_ref=left_ref.at[mine, :],
            send_sem=gather_send.at[step, piece],
            recv_sem=gather_recv.at[step, piece],
            device_id=(row, lax.rem(col - step + col_count, col_count)),
            device_id_type=MESH,
        )

    def arrival(step, piece):
        theirs = left_ref.at[rows_of(step, piece, 0), :]
        return pltpu.make_async_remote_copy(
            src_ref=theirs,
            dst_ref=theirs,
            send_sem=gather_send.at[step, piece],
            recv_sem=gather_recv.at[step, piece],
            device_id=(row, lax.rem(col - step + col_count, col_count)),
            device_id_type=MESH,
        )

    def ring(step, piece):
        held = right_ref.at[rows_of(step, piece, total), columns]
        return pltpu.make_async_remote_copy(
            src_ref=held,
            dst_ref=held,
            send_sem=ring_send.at[step, piece],
            recv_sem=ring_recv.at[step, piece],
            device_id=(next_row if (step + piece) % 2 == 0 else last_row, col),
            device_id_type=MESH,
        )

    def across(step, piece, hop, incoming):
        from_core = lax.rem(core + ratio - hop, ratio) if incoming else core
        there = pl.ds(pl.multiple_of(from_core * rows_tile, 128), rows_tile)
        held = right_ref.at[rows_of(step, piece, total), there]
        return pltpu.make_async_remote_copy(
            src_ref=held,
            dst_ref=held,
            send_sem=core_send.at[hop, step, piece],
            recv_sem=core_recv.at[hop, step, piece],
            device_id=(group * ratio + lax.rem(core + hop, ratio), col),
            device_id_type=MESH,
        )

    share = panel_ref.shape[0]

    def deal(step):
        taker = lax.rem(row - step + row_count, row_count)
        return pltpu.make_async_remote_copy(
            src_ref=panel_ref.at[:, pl.ds(pl.multiple_of(taker * rows_tile, 128), rows_tile)],
            dst_ref=left_ref.at[pl.ds(pl.multiple_of(total + row * share, 16), share), :],
            send_sem=deal_send.at[step],
            recv_sem=deal_recv.at[step],
            device_id=(taker, col),
            device_id_type=MESH,
        )

    def dealt(step):
        giver = lax.rem(row + step, row_count)
        theirs = left_ref.at[pl.ds(pl.multiple_of(total + giver * share, 16), share), :]
        return pltpu.make_async_remote_copy(
            src_ref=theirs,
            dst_ref=theirs,
            send_sem=deal_send.at[step],
            recv_sem=deal_recv.at[step],
            device_id=(giver, col),
            device_id_type=MESH,
        )

    for piece in range(PARTS):
        for step in range(1, col_count):
            gather(step, piece).start()
    for step in range(1, row_count):
        deal(step).start()
    own_rows = pl.ds(pl.multiple_of(col * depth, 16), depth)
    mine = panel_ref.at[:, pl.ds(pl.multiple_of(row * rows_tile, 128), rows_tile)]
    kept_rows = pl.ds(pl.multiple_of(total + row * share, 16), share)
    loads, stores = [], []
    for index, (source, held, target) in enumerate(
        (
            (block_ref, block_held, left_ref.at[own_rows, :]),
            (mine, own_held, left_ref.at[kept_rows, :]),
            (samples_ref, samples_held, right_ref.at[pl.ds(0, total), :]),
        )
    ):
        loads.append(pltpu.make_async_copy(source, held, load_sem.at[index]))
        stores.append(pltpu.make_async_copy(held, target, store_sem.at[index]))
    for copy in loads:
        copy.start()
    for load, store in zip(loads, stores):
        load.wait()
        store.start()

    for step in range(col_count):
        for piece in range(PARTS):
            travelled = behind if (step + piece) % 2 == 0 else ahead

            @pl.when(is_root)
            def _():
                if step == 0:
                    source = block_held.at[pl.ds(piece * part, part), :]
                else:
                    arrival(step, piece).wait_recv()
                    source = part_held
                    load = pltpu.make_async_copy(
                        left_ref.at[rows_of(step, piece, 0), :], part_held, step_sem.at[0]
                    )
                    load.start()
                    load.wait()
                store = pltpu.make_async_copy(
                    source, right_ref.at[rows_of(step, piece, total), columns], step_sem.at[1]
                )
                store.start()
                store.wait()

            @pl.when(jnp.logical_not(is_root))
            def _():
                ring(step, piece).wait_recv()

            @pl.when(travelled < groups - 1)
            def _():
                ring(step, piece).start()

            for hop in range(1, ratio):
                across(step, piece, hop, False).start()

    for step in range(col_count):
        for piece in range(PARTS):
            travelled = behind if (step + piece) % 2 == 0 else ahead

            @pl.when(travelled < groups - 1)
            def _():
                ring(step, piece).wait_send()

            if step:
                @pl.when(jnp.logical_not(is_root))
                def _():
                    arrival(step, piece).wait_recv()

                gather(step, piece).wait_send()
            for hop in range(1, ratio):
                across(step, piece, hop, False).wait_send()
                across(step, piece, hop, True).wait_recv()
    for step in range(1, row_count):
        deal(step).wait_send()
        dealt(step).wait_recv()
    for store in stores:
        store.wait()


def spread(block, panel, samples, row_count, col_count):
    total, cols_tile = samples.shape
    depth, rows_tile = block.shape
    share = panel.shape[0]
    ratio = row_count // col_count
    anywhere = pl.BlockSpec(memory_space=pl.ANY)
    pair = pltpu.SemaphoreType.DMA((col_count, PARTS))
    triple = pltpu.SemaphoreType.DMA((ratio, col_count, PARTS))
    return pl.pallas_call(
        functools.partial(spread_kernel, row_count, col_count),
        out_shape=(
            jax.ShapeDtypeStruct((2 * total, rows_tile), jnp.bfloat16),
            jax.ShapeDtypeStruct((2 * total, cols_tile), jnp.bfloat16),
        ),
        in_specs=[anywhere] * 3,
        out_specs=(anywhere, anywhere),
        scratch_shapes=[
            pair,
            pair,
            pair,
            pair,
            triple,
            triple,
            pltpu.SemaphoreType.DMA((row_count,)),
            pltpu.SemaphoreType.DMA((row_count,)),
            pltpu.SemaphoreType.DMA((3,)),
            pltpu.SemaphoreType.DMA((3,)),
            pltpu.SemaphoreType.DMA((2,)),
            pltpu.VMEM((depth, rows_tile), jnp.bfloat16),
            pltpu.VMEM((share, rows_tile), jnp.bfloat16),
            pltpu.VMEM((total, cols_tile), jnp.bfloat16),
            pltpu.VMEM((depth // PARTS, rows_tile), jnp.bfloat16),
        ],
        compiler_params=pltpu.CompilerParams(
            collective_id=0, has_side_effects=True, vmem_limit_bytes=40 * 2**20
        ),
    )(block, panel, samples)


def per_device(precision, samples, step_size, threshold):
    rows_tile, cols_tile = precision.shape
    sample_count = samples.shape[0]
    row_count, col_count = lax.axis_size("row"), lax.axis_size("col")
    row_index, col_index = lax.axis_index("row"), lax.axis_index("col")
    share = sample_count // row_count
    piece = lax.dynamic_slice_in_dim(samples, row_index * share, share, 0)
    panel = lax.all_gather(piece, "col", axis=1, tiled=True)

    depth = sample_count // col_count
    rounded = precision.astype(jnp.bfloat16)
    partial = lax.dot_general(
        samples, rounded, (((1,), (1,)), ((), ())), preferred_element_type=jnp.float32
    ).astype(jnp.bfloat16)
    terms = lax.all_to_all(
        partial.reshape(col_count, depth, rows_tile), "col", split_axis=0, concat_axis=0
    )
    block = jnp.sum(terms.astype(jnp.float32), axis=0).astype(jnp.bfloat16)

    left, right = spread(block, panel, samples, row_count, col_count)
    symmetric = lax.dot_general(
        left, right, (((0,), (0,)), ((), ())), preferred_element_type=jnp.float32
    ) * (0.5 / sample_count)
    global_row = row_index * rows_tile + jnp.arange(rows_tile, dtype=jnp.int32)
    global_col = col_index * cols_tile + jnp.arange(cols_tile, dtype=jnp.int32)
    on_diagonal = global_row[:, None] == global_col[None, :]
    gradient = symmetric - jnp.where(on_diagonal, 1.0 / jnp.where(on_diagonal, precision, 1.0), 0.0)
    stepped = precision - step_size[0] * gradient
    shrunk = jnp.sign(stepped) * jnp.maximum(jnp.abs(stepped) - step_size[0] * threshold[0], 0.0)
    return jnp.where(on_diagonal, stepped, shrunk)


def solution(mesh):
    in_specs = (P("row", "col"), P(None, "col"), P(), P())
    out_specs = P("row", "col")
    return jax.shard_map(
        per_device, mesh=mesh, in_specs=in_specs, out_specs=out_specs, check_vma=False
    )
```
